256 devices in a mesh: gy: 16 (over z, core), gx: 16 (over y, x).
Axes of the slice: x: 4, y: 4, z: 8, core: 2. Of those that a mesh axis runs over, the one named last changes fastest.
Arguments:
- embedding: bfloat16 [16, 6, 1024, 4096], P(None, None, 'gy', 'gx'), may hold values from -4 to 4
- offsets: int32 [12, 3], replicated, may hold values from -27 to 27, as said below
- targets: int32 [6, 1024, 4096], P(None, 'gy', 'gx'), may hold values from 0 to 4095
- mask: int32 [6, 1024, 4096], P(None, 'gy', 'gx'), may hold values 0 or 1
Outputs:
- embed_grad: float32 [16, 6, 1024, 4096], P(None, None, 'gy', 'gx')
The draws below stay inside these ranges and needn't reach their ends.
Inputs may be any that keep to these rules, and one draw needn't show every extreme that they name: `offsets`: each row is (z, y, x) with |z| <= 3 and |y|, |x| <= 27, never all zero; row 0 has y = 27, row 1 has x = -27, row 2 has z = 3.
All inputs are finite; a program needn't handle non-finite values. No bound on the sum of `mask` on one device may be relied on, other than what follows from the above.
Results may differ from the reference program's by a relative error of at most 0.0006.
Values may be sent and summed in bfloat16 or wider, within the bound.
A program may use at most 192 MiB of HBM per device.

```python
import jax
import jax.numpy as jnp
from jax import lax

C = 16
K = 12
REACH = 27
ZR = 3
Z = 6
NY = 1024
NX = 4096


def draw_offsets(key, part):
    key = jax.random.fold_in(key, 7)
    key_z, key_y, key_x = jax.random.split(key, 3)
    shift_z = jax.random.randint(key_z, (K,), -ZR, ZR + 1).astype(jnp.int32)
    shift_y = jax.random.randint(key_y, (K,), -REACH, REACH + 1).astype(jnp.int32)
    shift_x = jax.random.randint(key_x, (K,), -REACH, REACH + 1).astype(jnp.int32)
    shift_y = shift_y.at[0].set(REACH)
    shift_x = shift_x.at[1].set(-REACH)
    shift_z = shift_z.at[2].set(ZR)
    shift_y = jnp.where((shift_z == 0) & (shift_y == 0) & (shift_x == 0), 1, shift_y)
    return jnp.stack([shift_z, shift_y, shift_x], axis=1).astype(jnp.int32)


def touch_ends(drawn, stream_key, smallest, high):
    index_at = [jax.random.randint(jax.random.fold_in(stream_key, axis), (), 0, length) for axis, length in enumerate(drawn.shape)]
    widest = drawn.shape.index(max(drawn.shape))
    neighbour = index_at[:widest] + [(index_at[widest] + 1) % drawn.shape[widest]] + index_at[widest + 1:]
    return drawn.at[tuple(index_at)].set(smallest).at[tuple(neighbour)].set(high)


def levels(rng, extent, shards, least, high):
    def one(dim, parts):
        heights = jax.random.uniform(jax.random.fold_in(jax.random.fold_in(rng, 6), dim), (parts,), jnp.float32, least / len(shards), high / len(shards))
        return jnp.repeat(jnp.exp(heights), extent[dim] // parts).reshape((-1,) + (1,) * (len(extent) - dim - 1))

    factor_of = one(*shards[0])
    for cut in shards[1:]:
        factor_of = factor_of * one(*cut)
    return factor_of


def scatter_about(rng, dims, scale, limit, cuts=(), kind=jnp.bfloat16):
    factor_of = levels(rng, dims, cuts, -0.22, 0.18) if cuts else 1.0
    result = jax.random.normal(rng, dims, jnp.float32) * scale * factor_of
    return jnp.minimum(jnp.maximum(result, -limit), limit).astype(kind)


def setup_inputs(seed: int = 0) -> dict:
    key_of = jax.random.split(jax.random.key(seed), 5)
    embedding = scatter_about(key_of[0], (C, Z, NY, NX), 0.5, 4.0, ((2, 16), (3, 16)))
    offsets = draw_offsets(jax.random.fold_in(key_of[4], 71), 0)
    targets = touch_ends(jax.random.randint(key_of[2], (Z, NY, NX), 0, 4096), jax.random.fold_in(key_of[2], 1), 0, 4095).astype(jnp.int32)
    mask = touch_ends((jax.random.randint(key_of[3], (Z, NY, NX), 0, 4) < 3).astype(jnp.int32), jax.random.fold_in(key_of[3], 1), 0, 1)
    return dict(embedding=embedding, offsets=offsets, targets=targets, mask=mask)


def reference(embedding, offsets, targets, mask):
    embed_float = embedding.astype(jnp.float32)
    padded = jnp.pad(embed_float, ((0, 0), (ZR, ZR), (REACH, REACH), (REACH, REACH)))
    z_index = jnp.arange(Z).astype(jnp.int32)[:, None, None]
    y_index = jnp.arange(NY).astype(jnp.int32)[None, :, None]
    x_index = jnp.arange(NX).astype(jnp.int32)[None, None, :]
    keep_mask = mask.astype(jnp.float32)

    def offset_step(which, state_pair):
        own_grad, returned = state_pair
        which = which.astype(jnp.int32)
        shift_z = offsets[which, 0].astype(jnp.int32)
        shift_y = offsets[which, 1].astype(jnp.int32)
        shift_x = offsets[which, 2].astype(jnp.int32)
        anchor = (jnp.int32(0), (ZR + shift_z).astype(jnp.int32), (REACH + shift_y).astype(jnp.int32), (REACH + shift_x).astype(jnp.int32))
        partner = lax.dynamic_slice(padded, anchor, (C, Z, NY, NX))
        logits = jnp.sum(embed_float * partner, axis=0)
        inside = ((z_index + shift_z >= 0) & (z_index + shift_z < Z) & (y_index + shift_y >= 0) & (y_index + shift_y < NY) & (x_index + shift_x >= 0) & (x_index + shift_x < NX))
        target_bit = jnp.bitwise_and(jnp.right_shift(targets, which), 1).astype(jnp.float32)
        slope = keep_mask * inside.astype(jnp.float32) * (jax.nn.sigmoid(logits) - target_bit)
        own_grad = own_grad + slope[None] * partner
        region = lax.dynamic_slice(returned, anchor, (C, Z, NY, NX))
        returned = lax.dynamic_update_slice(returned, region + slope[None] * embed_float, anchor)
        return own_grad, returned

    own_grad = jnp.zeros((C, Z, NY, NX), jnp.float32)
    returned = jnp.zeros(padded.shape, jnp.float32)
    own_grad, returned = lax.fori_loop(0, K, offset_step, (own_grad, returned))
    return own_grad + returned[:, ZR:ZR + Z, REACH:REACH + NY, REACH:REACH + NX]
```

```python
import functools

import jax
import jax.numpy as jnp
from jax import lax
from jax.experimental import pallas as pl
from jax.experimental.pallas import tpu as pltpu
from jax.sharding import PartitionSpec as P

HALO = 32
LANES = 128
SLOTS = LANES // HALO
LOW = 64
VMEM_BYTES = 56 << 20


def roll_to(value, source, dest):
    return value if source == dest else pltpu.roll(value, (dest - source) % LANES, 1)


def pack_kernel(e_ref, t_ref, m_ref, own_ref, first_ref, last_ref):
    channels, slices, rows, _ = e_ref.shape
    planes = channels + 2
    lane = lax.broadcasted_iota(jnp.int32, (rows, LANES), 1)
    for z in range(slices):
        for x in range(2):
            cols = slice(x * LANES, (x + 1) * LANES)
            for c in range(channels):
                own_ref[x, z, c] = e_ref[c, z, :, cols]
            code = t_ref[z, :, cols] | jnp.left_shift(m_ref[z, :, cols], 12)
            own_ref[x, z, channels] = (code & (LOW - 1)).astype(jnp.float32).astype(jnp.bfloat16)
            own_ref[x, z, channels + 1] = jnp.right_shift(code, 6).astype(jnp.float32).astype(jnp.bfloat16)
    for group in range(slices * planes // SLOTS):
        for x, out in ((0, first_ref), (1, last_ref)):
            packed = None
            for slot in range(SLOTS):
                z, c = divmod(group * SLOTS + slot, planes)
                moved = roll_to(own_ref[x, z, c], x * (LANES - HALO), slot * HALO)
                packed = moved if packed is None else jnp.where(lane >= slot * HALO, moved, packed)
            out[group] = packed


def pack(embedding, targets, mask):
    channels, slices, rows, cols = embedding.shape
    planes = channels + 2
    strip = jax.ShapeDtypeStruct((slices * planes // SLOTS, rows, LANES), jnp.bfloat16)
    return pl.pallas_call(
        pack_kernel,
        out_shape=(jax.ShapeDtypeStruct((2, slices, planes, rows, LANES), jnp.bfloat16), strip, strip),
        compiler_params=pltpu.CompilerParams(vmem_limit_bytes=VMEM_BYTES),
        name="pack",
    )(embedding, targets, mask)


def affinity_kernel(off_ref, own_ref, above_ref, below_ref, right_ref, left_ref, ra_ref, la_ref, rb_ref, lb_ref,
                    g_ref, f_ref, t_ref, m_ref, w_ref, *, per):
    _, nz, planes, own_rows, _ = own_ref.shape
    nc = planes - 2
    tiles = own_rows // 8
    lane = lax.broadcasted_iota(jnp.int32, (8, 128), 1)
    spans = (
        (0, HALO, above_ref, ra_ref, la_ref),
        (HALO, own_rows, own_ref, right_ref, left_ref),
        (HALO + own_rows, HALO, below_ref, rb_ref, lb_ref),
    )

    def decode(blk, z, at, low, high):
        code = (low.astype(jnp.float32) + LOW * high.astype(jnp.float32)).astype(jnp.int32)
        t_ref[blk, z, at, :] = code
        m_ref[blk, z, at, :] = jnp.right_shift(code, 12).astype(jnp.float32)

    for start, size, body_ref, r_ref, l_ref in spans:
        at = slice(start, start + size)
        wide = lax.broadcasted_iota(jnp.int32, (size, LANES), 1)

        def cast(z, _):
            for x in range(2):
                f_ref[1 + x, z, :, at, :] = body_ref[x, z, :nc].astype(jnp.float32)
                decode(1 + x, z, at, body_ref[x, z, nc], body_ref[x, z, nc + 1])
            return 0
        lax.fori_loop(0, nz, cast, 0)
        for z in range(nz):
            held = []
            for c in range(planes):
                group, slot = divmod(z * planes + c, SLOTS)
                from_right = roll_to(r_ref[group], slot * HALO, 0)
                from_left = roll_to(l_ref[group], slot * HALO, LANES - HALO)
                halo = jnp.where(wide < LANES // 2, from_right, from_left)
                if c < nc:
                    f_ref[0, z, c, at, :] = halo.astype(jnp.float32)
                else:
                    held.append(halo)
            decode(0, z, at, *held)

    rows = lax.broadcasted_iota(jnp.int32, (256, 256), 0)
    cols = lax.broadcasted_iota(jnp.int32, (256, 256), 1)

    def zero(i, _):
        g_ref[i] = jnp.zeros(g_ref.shape[1:], jnp.float32)
        return 0
    lax.fori_loop(0, nc, zero, 0)

    def pair(k, _):
        oz, oy, ox = off_ref[k, 0], off_ref[k, 1], off_ref[k, 2]
        bit = jnp.left_shift(1, k)
        lo = jnp.maximum(0, -oz)
        hi = jnp.minimum(nz, nz - oz)

        def shifted(slot, dx):
            w_ref[slot] = jnp.where(rows == ((cols + dx) & 255), 1.0, 0.0).astype(jnp.bfloat16)
            in0 = lane < dx
            in1 = lane >= 128 + dx
            def merge(h, a, b):
                return jnp.concatenate([jnp.where(in0, h, a), jnp.where(in1, h, b)], axis=1)
            return merge
        merge_f = shifted(0, ox)
        merge_b = shifted(1, -ox)

        def label(z, r0, blk):
            m = m_ref[blk, z, pl.ds(r0, 8), :]
            t = t_ref[blk, z, pl.ds(r0, 8), :]
            return jnp.where((t & bit) != 0, -m, m)

        def tile(t, own, src, dy, merge, slot, back):
            r0 = 32 + dy + t * 8
            parts = [merge(*(f_ref[blk, src, c, pl.ds(r0, 8), :] for blk in range(3))) for c in range(nc)]
            if back:
                lab = merge(*(label(src, r0, blk) for blk in range(3)))
                parts += [lab, lab]
            lhs = jnp.concatenate(parts, axis=0).astype(jnp.bfloat16)
            p = jnp.dot(lhs, w_ref[slot], preferred_element_type=jnp.float32)
            o0 = 32 + t * 8
            for x in range(2):
                xs = slice(x * 128, x * 128 + 128)
                q = [p[c * 8:c * 8 + 8, xs] for c in range(nc)]
                prods = [q[c] * f_ref[1 + x, own, c, o0:o0 + 8, :] for c in range(nc)]
                while len(prods) > 1:
                    prods = [u + v for u, v in zip(prods[::2], prods[1::2])]
                if back:
                    lab = p[nc * 8:nc * 8 + 8, xs]
                    keep = jnp.abs(lab)
                else:
                    lab = label(own, o0, 1 + x)
                    keep = m_ref[1 + x, own, o0:o0 + 8, :]
                s = keep * jnp.tanh(prods[0] * 0.5) + lab
                for c in range(nc):
                    g_ref[c, own, t * 8:t * 8 + 8, xs] += s * q[c]

        def plane(z, _):
            for t in range(0, tiles, per):
                for i in range(t, t + per):
                    tile(i, z, z + oz, oy, merge_f, 0, False)
                for i in range(t, t + per):
                    tile(i, z + oz, z, -oy, merge_b, 1, True)
            return 0
        lax.fori_loop(lo, hi, plane, 0)
        return 0
    lax.fori_loop(0, off_ref.shape[0], pair, 0)

    def half(i, _):
        g_ref[i] = g_ref[i] * 0.5
        return 0
    lax.fori_loop(0, nc, half, 0)


def affinity(off, own, *halos):
    _, nz, planes, rows, _ = own.shape
    nc = planes - 2
    V = pl.BlockSpec(memory_space=pltpu.VMEM)
    tall = rows + 2 * HALO
    return pl.pallas_call(
        functools.partial(affinity_kernel, per=8),
        out_shape=jax.ShapeDtypeStruct((nc, nz, rows, 2 * LANES), jnp.float32),
        in_specs=[pl.BlockSpec(memory_space=pltpu.SMEM)] + [V] * (1 + len(halos)),
        out_specs=V,
        scratch_shapes=[
            pltpu.VMEM((3, nz, nc, tall, LANES), jnp.float32),
            pltpu.VMEM((3, nz, tall, LANES), jnp.int32),
            pltpu.VMEM((3, nz, tall, LANES), jnp.float32),
            pltpu.VMEM((2, 256, 256), jnp.bfloat16),
        ],
        compiler_params=pltpu.CompilerParams(vmem_limit_bytes=VMEM_BYTES),
        name="affinity",
    )(off, own, *halos)


def send(value, axis, step):
    count = lax.axis_size(axis)
    return lax.ppermute(value, axis, [(i, i + step) for i in range(count) if 0 <= i + step < count])


def on_device(embedding, offsets, targets, mask):
    rows = embedding.shape[2]
    own, first, last = pack(embedding, targets, mask)
    from_above = send(own[..., rows - HALO:, :], "gy", 1)
    from_below = send(own[..., :HALO, :], "gy", -1)
    right = send(first, "gx", -1)
    left = send(last, "gx", 1)
    corners_above = [send(v[:, rows - HALO:], "gy", 1) for v in (right, left)]
    corners_below = [send(v[:, :HALO], "gy", -1) for v in (right, left)]
    return affinity(offsets, own, from_above, from_below, right, left, *corners_above, *corners_below)


def solution(mesh):
    return jax.shard_map(
        on_device,
        mesh=mesh,
        in_specs=(P(None, None, "gy", "gx"), P(), P(None, "gy", "gx"), P(None, "gy", "gx")),
        out_specs=P(None, None, "gy", "gx"),
        check_vma=False,
    )
```

```python
import functools

import jax
import jax.numpy as jnp
from jax import lax
from jax.experimental import pallas as pl
from jax.experimental.pallas import tpu as pltpu
from jax.sharding import PartitionSpec as P

MESH = pl.DeviceIdType.MESH
HALO = 32
LANES = 128
SLOTS = LANES // HALO
LOW = 64
VMEM_BYTES = 56 << 20


def roll_to(value, source, dest):
    return value if source == dest else pltpu.roll(value, (dest - source) % LANES, 1)


def exchange_kernel(e_ref, t_ref, m_ref, body_ref, side_ref, strip_ref, copied, sent, received):
    channels, slices, rows, _ = e_ref.shape
    planes = channels + 2
    groups = strip_ref.shape[1]
    me_y, me_x = lax.axis_index("gy"), lax.axis_index("gx")
    count_y, count_x = lax.axis_size("gy"), lax.axis_size("gx")
    below, above = (lax.rem(me_y + 1, count_y), me_x), (lax.rem(me_y + count_y - 1, count_y), me_x)
    right, left = (me_y, lax.rem(me_x + 1, count_x)), (me_y, lax.rem(me_x + count_x - 1, count_x))
    mine, tail, head = pl.ds(HALO, rows), pl.ds(rows, HALO), pl.ds(HALO, HALO)
    top, bottom = pl.ds(0, HALO), pl.ds(HALO + rows, HALO)

    own = [
        pltpu.make_async_copy(
            e_ref.at[:, :, :, pl.ds(x * LANES, LANES)], body_ref.at[x, pl.ds(0, channels), :, mine], copied.at[x]
        )
        for x in range(2)
    ]
    for copy in own:
        copy.start()

    barrier = pltpu.get_barrier_semaphore()
    for neighbour in (below, above, right, left):
        pl.semaphore_signal(barrier, inc=1, device_id=neighbour, device_id_type=MESH)
    pl.semaphore_wait(barrier, 4)

    def remote(index, source, target, device):
        copy = pltpu.make_async_remote_copy(
            src_ref=source, dst_ref=target, send_sem=sent.at[index], recv_sem=received.at[index],
            device_id=device, device_id_type=MESH,
        )
        copy.start()
        return copy

    inner = pl.ds(0, channels)
    flights = []
    for x in range(2):
        cols = pl.ds(x * LANES, LANES)
        flights.append(remote(x, e_ref.at[:, :, pl.ds(rows - HALO, HALO), cols], body_ref.at[x, inner, :, top], below))
        flights.append(remote(2 + x, e_ref.at[:, :, pl.ds(0, HALO), cols], body_ref.at[x, inner, :, bottom], above))

    for z in range(slices):
        for x in range(2):
            cols = slice(x * LANES, (x + 1) * LANES)
            code = t_ref[z, :, cols] | jnp.left_shift(m_ref[z, :, cols], 12)
            body_ref[x, channels, z, HALO:HALO + rows] = (code & (LOW - 1)).astype(jnp.float32).astype(jnp.bfloat16)
            body_ref[x, channels + 1, z, HALO:HALO + rows] = jnp.right_shift(code, 6).astype(jnp.float32).astype(jnp.bfloat16)
    codes = pl.ds(channels, 2)
    flights.append(remote(4, body_ref.at[:, codes, :, tail], body_ref.at[:, codes, :, top], below))
    flights.append(remote(5, body_ref.at[:, codes, :, head], body_ref.at[:, codes, :, bottom], above))

    for copy in own:
        copy.wait()
    lane = lax.broadcasted_iota(jnp.int32, (rows, LANES), 1)
    across = []
    for x, device in ((1, right), (0, left)):
        for group in range(groups):
            packed = None
            for slot in range(SLOTS):
                c, z = divmod(group * SLOTS + slot, slices)
                moved = roll_to(body_ref[x, c, z, HALO:HALO + rows], x * (LANES - HALO), slot * HALO)
                packed = moved if packed is None else jnp.where(lane >= slot * HALO, moved, packed)
            strip_ref[x, group] = packed
        across.append(remote(6 + x, strip_ref.at[x], side_ref.at[x, :, mine], device))
    for copy in across:
        copy.wait()

    corners = [
        remote(8, side_ref.at[:, :, tail], side_ref.at[:, :, top], below),
        remote(9, side_ref.at[:, :, head], side_ref.at[:, :, bottom], above),
    ]
    for copy in flights + corners:
        copy.wait()

    @pl.when(me_y == 0)
    def _():
        body_ref[:, :, :, 0:HALO] = jnp.zeros((2, planes, slices, HALO, LANES), jnp.bfloat16)
        side_ref[:, :, 0:HALO] = jnp.zeros((2, groups, HALO, LANES), jnp.bfloat16)

    @pl.when(me_y == count_y - 1)
    def _():
        body_ref[:, :, :, HALO + rows:] = jnp.zeros((2, planes, slices, HALO, LANES), jnp.bfloat16)
        side_ref[:, :, HALO + rows:] = jnp.zeros((2, groups, HALO, LANES), jnp.bfloat16)

    @pl.when(me_x == 0)
    def _():
        side_ref[1] = jnp.zeros(side_ref.shape[1:], jnp.bfloat16)

    @pl.when(me_x == count_x - 1)
    def _():
        side_ref[0] = jnp.zeros(side_ref.shape[1:], jnp.bfloat16)


def exchange(embedding, targets, mask):
    channels, slices, rows, cols = embedding.shape
    planes = channels + 2
    groups = slices * planes // SLOTS
    tall = rows + 2 * HALO
    V = pl.BlockSpec(memory_space=pltpu.VMEM)
    return pl.pallas_call(
        exchange_kernel,
        out_shape=(
            jax.ShapeDtypeStruct((2, planes, slices, tall, LANES), jnp.bfloat16),
            jax.ShapeDtypeStruct((2, groups, tall, LANES), jnp.bfloat16),
        ),
        in_specs=[pl.BlockSpec(memory_space=pl.ANY), V, V],
        out_specs=(V, V),
        scratch_shapes=[
            pltpu.VMEM((2, groups, rows, LANES), jnp.bfloat16),
            pltpu.SemaphoreType.DMA((2,)),
            pltpu.SemaphoreType.DMA((10,)),
            pltpu.SemaphoreType.DMA((10,)),
        ],
        compiler_params=pltpu.CompilerParams(
            collective_id=0, has_side_effects=True, vmem_limit_bytes=VMEM_BYTES
        ),
        name="exchange",
    )(embedding, targets, mask)


def affinity_kernel(off_ref, body_ref, side_ref, g_ref, f_ref, t_ref, m_ref, w_ref, *, per):
    _, planes, nz, tall, _ = body_ref.shape
    nc = planes - 2
    tiles = (tall - 2 * HALO) // 8
    lane = lax.broadcasted_iota(jnp.int32, (8, 128), 1)
    wide = lax.broadcasted_iota(jnp.int32, (tall, LANES), 1)

    def halo(c, z):
        group, slot = divmod(c * nz + z, SLOTS)
        from_right = roll_to(side_ref[0, group], slot * HALO, 0)
        from_left = roll_to(side_ref[1, group], slot * HALO, LANES - HALO)
        return jnp.where(wide < LANES // 2, from_right, from_left)

    def decode(blk, z, low, high):
        code = (low.astype(jnp.float32) + LOW * high.astype(jnp.float32)).astype(jnp.int32)
        t_ref[blk, z] = code
        m_ref[blk, z] = jnp.right_shift(code, 12).astype(jnp.float32)

    def cast(c, _):
        for x in range(2):
            f_ref[1 + x, c] = body_ref[x, c].astype(jnp.float32)
        return 0
    lax.fori_loop(0, nc, cast, 0)
    for c in range(nc):
        for z in range(nz):
            f_ref[0, c, z] = halo(c, z).astype(jnp.float32)
    for z in range(nz):
        for x in range(2):
            decode(1 + x, z, body_ref[x, nc, z], body_ref[x, nc + 1, z])
        decode(0, z, halo(nc, z), halo(nc + 1, z))

    rows = lax.broadcasted_iota(jnp.int32, (256, 256), 0)
    cols = lax.broadcasted_iota(jnp.int32, (256, 256), 1)

    def zero(i, _):
        g_ref[i] = jnp.zeros(g_ref.shape[1:], jnp.float32)
        return 0
    lax.fori_loop(0, nc, zero, 0)

    def pair(k, _):
        oz, oy, ox = off_ref[k, 0], off_ref[k, 1], off_ref[k, 2]
        bit = jnp.left_shift(1, k)
        lo = jnp.maximum(0, -oz)
        hi = jnp.minimum(nz, nz - oz)

        def shifted(slot, dx):
            w_ref[slot] = jnp.where(rows == ((cols + dx) & 255), 1.0, 0.0).astype(jnp.bfloat16)
            in0 = lane < dx
            in1 = lane >= 128 + dx
            def merge(h, a, b):
                return jnp.concatenate([jnp.where(in0, h, a), jnp.where(in1, h, b)], axis=1)
            return merge
        merge_f = shifted(0, ox)
        merge_b = shifted(1, -ox)

        def label(z, r0, blk):
            m = m_ref[blk, z, pl.ds(r0, 8), :]
            t = t_ref[blk, z, pl.ds(r0, 8), :]
            return jnp.where((t & bit) != 0, -m, m)

        def tile(t, own, src, dy, merge, slot, back):
            r0 = 32 + dy + t * 8
            parts = [merge(*(f_ref[blk, c, src, pl.ds(r0, 8), :] for blk in range(3))) for c in range(nc)]
            if back:
                lab = merge(*(label(src, r0, blk) for blk in range(3)))
                parts += [lab, lab]
            lhs = jnp.concatenate(parts, axis=0).astype(jnp.bfloat16)
            p = jnp.dot(lhs, w_ref[slot], preferred_element_type=jnp.float32)
            o0 = 32 + t * 8
            for x in range(2):
                xs = slice(x * 128, x * 128 + 128)
                q = [p[c * 8:c * 8 + 8, xs] for c in range(nc)]
                prods = [q[c] * f_ref[1 + x, c, own, o0:o0 + 8, :] for c in range(nc)]
                while len(prods) > 1:
                    prods = [u + v for u, v in zip(prods[::2], prods[1::2])]
                if back:
                    lab = p[nc * 8:nc * 8 + 8, xs]
                    keep = jnp.abs(lab)
                else:
                    lab = label(own, o0, 1 + x)
                    keep = m_ref[1 + x, own, o0:o0 + 8, :]
                s = keep * jnp.tanh(prods[0] * 0.5) + lab
                for c in range(nc):
                    g_ref[c, own, t * 8:t * 8 + 8, xs] += s * q[c]

        def plane(z, _):
            for t in range(0, tiles, per):
                for i in range(t, t + per):
                    tile(i, z, z + oz, oy, merge_f, 0, False)
                for i in range(t, t + per):
                    tile(i, z + oz, z, -oy, merge_b, 1, True)
            return 0
        lax.fori_loop(lo, hi, plane, 0)
        return 0
    lax.fori_loop(0, off_ref.shape[0], pair, 0)

    def half(i, _):
        g_ref[i] = g_ref[i] * 0.5
        return 0
    lax.fori_loop(0, nc, half, 0)


def affinity(off, body, side):
    _, planes, nz, tall, _ = body.shape
    nc = planes - 2
    V = pl.BlockSpec(memory_space=pltpu.VMEM)
    return pl.pallas_call(
        functools.partial(affinity_kernel, per=8),
        out_shape=jax.ShapeDtypeStruct((nc, nz, tall - 2 * HALO, 2 * LANES), jnp.float32),
        in_specs=[pl.BlockSpec(memory_space=pltpu.SMEM), V, V],
        out_specs=V,
        scratch_shapes=[
            pltpu.VMEM((3, nc, nz, tall, LANES), jnp.float32),
            pltpu.VMEM((3, nz, tall, LANES), jnp.int32),
            pltpu.VMEM((3, nz, tall, LANES), jnp.float32),
            pltpu.VMEM((2, 256, 256), jnp.bfloat16),
        ],
        compiler_params=pltpu.CompilerParams(vmem_limit_bytes=VMEM_BYTES),
        name="affinity",
    )(off, body, side)


def on_device(embedding, offsets, targets, mask):
    return affinity(offsets, *exchange(embedding, targets, mask))


def solution(mesh):
    return jax.shard_map(
        on_device,
        mesh=mesh,
        in_specs=(P(None, None, "gy", "gx"), P(), P(None, "gy", "gx"), P(None, "gy", "gx")),
        out_specs=P(None, None, "gy", "gx"),
        check_vma=False,
    )
```

```python
import jax
import jax.numpy as jnp
from jax import lax
from jax.experimental import pallas as pl
from jax.experimental.pallas import tpu as pltpu
from jax.sharding import PartitionSpec as P

MESH = pl.DeviceIdType.MESH
HALO = 32
LANES = 128
SLOTS = LANES // HALO
LOW = 64
VMEM_BYTES = 58 << 20
PAD = 8


def roll_to(value, source, dest):
    return value if source == dest else pltpu.roll(value, (dest - source) % LANES, 1)


def exchange_kernel(e_ref, t_ref, m_ref, body_ref, side_ref, strip_ref, copied, sent, received):
    channels, slices, rows, _ = e_ref.shape
    planes = channels + 2
    groups = strip_ref.shape[1]
    me_y, me_x = lax.axis_index("gy"), lax.axis_index("gx")
    count_y, count_x = lax.axis_size("gy"), lax.axis_size("gx")
    below, above = (lax.rem(me_y + 1, count_y), me_x), (lax.rem(me_y + count_y - 1, count_y), me_x)
    right, left = (me_y, lax.rem(me_x + 1, count_x)), (me_y, lax.rem(me_x + count_x - 1, count_x))
    mine, tail, head = pl.ds(HALO, rows), pl.ds(rows, HALO), pl.ds(HALO, HALO)
    top, bottom = pl.ds(0, HALO), pl.ds(HALO + rows, HALO)

    own = [
        pltpu.make_async_copy(
            e_ref.at[:, :, :, pl.ds(x * LANES, LANES)], body_ref.at[x, pl.ds(0, channels), :, mine], copied.at[x]
        )
        for x in range(2)
    ]
    for copy in own:
        copy.start()

    barrier = pltpu.get_barrier_semaphore()
    for neighbour in (below, above, right, left):
        pl.semaphore_signal(barrier, inc=1, device_id=neighbour, device_id_type=MESH)
    pl.semaphore_wait(barrier, 4)

    def remote(index, source, target, device):
        copy = pltpu.make_async_remote_copy(
            src_ref=source, dst_ref=target, send_sem=sent.at[index], recv_sem=received.at[index],
            device_id=device, device_id_type=MESH,
        )
        copy.start()
        return copy

    inner = pl.ds(0, channels)
    flights = []
    for x in range(2):
        cols = pl.ds(x * LANES, LANES)
        flights.append(remote(x, e_ref.at[:, :, pl.ds(rows - HALO, HALO), cols], body_ref.at[x, inner, :, top], below))
        flights.append(remote(2 + x, e_ref.at[:, :, pl.ds(0, HALO), cols], body_ref.at[x, inner, :, bottom], above))

    for z in range(slices):
        for x in range(2):
            cols = slice(x * LANES, (x + 1) * LANES)
            code = t_ref[z, :, cols] | jnp.left_shift(m_ref[z, :, cols], 12)
            body_ref[x, channels, z, HALO:HALO + rows] = (code & (LOW - 1)).astype(jnp.float32).astype(jnp.bfloat16)
            body_ref[x, channels + 1, z, HALO:HALO + rows] = jnp.right_shift(code, 6).astype(jnp.float32).astype(jnp.bfloat16)
    codes = pl.ds(channels, 2)
    flights.append(remote(4, body_ref.at[:, codes, :, tail], body_ref.at[:, codes, :, top], below))
    flights.append(remote(5, body_ref.at[:, codes, :, head], body_ref.at[:, codes, :, bottom], above))

    for copy in own:
        copy.wait()
    lane = lax.broadcasted_iota(jnp.int32, (rows, LANES), 1)
    across = []
    for x, device in ((1, right), (0, left)):
        for group in range(groups):
            packed = None
            for slot in range(SLOTS):
                c, z = divmod(group * SLOTS + slot, slices)
                moved = roll_to(body_ref[x, c, z, HALO:HALO + rows], x * (LANES - HALO), slot * HALO)
                packed = moved if packed is None else jnp.where(lane >= slot * HALO, moved, packed)
            strip_ref[x, group] = packed
        across.append(remote(6 + x, strip_ref.at[x], side_ref.at[x, :, mine], device))
    for copy in across:
        copy.wait()

    corners = [
        remote(8, side_ref.at[:, :, tail], side_ref.at[:, :, top], below),
        remote(9, side_ref.at[:, :, head], side_ref.at[:, :, bottom], above),
    ]
    for copy in flights + corners:
        copy.wait()

    @pl.when(me_y == 0)
    def _():
        body_ref[:, :, :, 0:HALO] = jnp.zeros((2, planes, slices, HALO, LANES), jnp.bfloat16)
        side_ref[:, :, 0:HALO] = jnp.zeros((2, groups, HALO, LANES), jnp.bfloat16)

    @pl.when(me_y == count_y - 1)
    def _():
        body_ref[:, :, :, HALO + rows:] = jnp.zeros((2, planes, slices, HALO, LANES), jnp.bfloat16)
        side_ref[:, :, HALO + rows:] = jnp.zeros((2, groups, HALO, LANES), jnp.bfloat16)

    @pl.when(me_x == 0)
    def _():
        side_ref[1] = jnp.zeros(side_ref.shape[1:], jnp.bfloat16)

    @pl.when(me_x == count_x - 1)
    def _():
        side_ref[0] = jnp.zeros(side_ref.shape[1:], jnp.bfloat16)


def exchange(embedding, targets, mask):
    channels, slices, rows, cols = embedding.shape
    planes = channels + 2
    groups = slices * planes // SLOTS
    tall = rows + 2 * HALO
    V = pl.BlockSpec(memory_space=pltpu.VMEM)
    return pl.pallas_call(
        exchange_kernel,
        out_shape=(
            jax.ShapeDtypeStruct((2, planes, slices, tall, LANES), jnp.bfloat16),
            jax.ShapeDtypeStruct((2, groups, tall, LANES), jnp.bfloat16),
        ),
        in_specs=[pl.BlockSpec(memory_space=pl.ANY), V, V],
        out_specs=(V, V),
        scratch_shapes=[
            pltpu.VMEM((2, groups, rows, LANES), jnp.bfloat16),
            pltpu.SemaphoreType.DMA((2,)),
            pltpu.SemaphoreType.DMA((10,)),
            pltpu.SemaphoreType.DMA((10,)),
        ],
        compiler_params=pltpu.CompilerParams(
            collective_id=0, has_side_effects=True, vmem_limit_bytes=VMEM_BYTES
        ),
        name="exchange",
    )(embedding, targets, mask)


def affinity_kernel(off_ref, body_ref, side_ref, g_ref, f_ref, t_ref, m_ref, gf_ref, gb_ref):
    _, planes, nz, tall, _ = body_ref.shape
    nc = planes - 2
    tiles = (tall - 2 * HALO) // 8
    lane = lax.broadcasted_iota(jnp.int32, (8, 128), 1)
    wide = lax.broadcasted_iota(jnp.int32, (tall, LANES), 1)

    def halo(c, z):
        group, slot = divmod(c * nz + z, SLOTS)
        from_right = roll_to(side_ref[0, group], slot * HALO, 0)
        from_left = roll_to(side_ref[1, group], slot * HALO, LANES - HALO)
        return jnp.where(wide < LANES // 2, from_right, from_left)

    def decode(blk, z, low, high):
        code = (low.astype(jnp.float32) + LOW * high.astype(jnp.float32)).astype(jnp.int32)
        t_ref[blk, z] = code
        m_ref[blk, z] = jnp.right_shift(code, 12).astype(jnp.float32)

    def cast(c, _):
        for x in range(2):
            for z in range(nz):
                f_ref[1 + x, z, c, :tall] = body_ref[x, c, z].astype(jnp.float32)
        return 0
    lax.fori_loop(0, nc, cast, 0)
    for c in range(nc):
        for z in range(nz):
            f_ref[0, z, c, :tall] = halo(c, z).astype(jnp.float32)
    for z in range(nz):
        for x in range(2):
            decode(1 + x, z, body_ref[x, nc, z], body_ref[x, nc + 1, z])
        decode(0, z, halo(nc, z), halo(nc + 1, z))

    def zero(c, _):
        gf_ref[c] = jnp.zeros(gf_ref.shape[1:], jnp.float32)
        gb_ref[c] = jnp.zeros(gb_ref.shape[1:], jnp.float32)
        return 0
    lax.fori_loop(0, nc, zero, 0)

    rows = lax.broadcasted_iota(jnp.int32, (256, 256), 0)
    cols = lax.broadcasted_iota(jnp.int32, (256, 256), 1)

    def pair(k, acc_f, acc_b):
        oz, oy, ox = off_ref[k, 0], off_ref[k, 1], off_ref[k, 2]
        bit = jnp.left_shift(1, k)
        lo = jnp.maximum(0, -oz)
        hi = jnp.minimum(nz, nz - oz)
        steps = tiles // 2

        def columns(dx):
            edge = jnp.where(dx > 0, 1, 2)
            flip = jnp.where(dx > 0, 0, 128)
            weight = jnp.where(rows == (((cols + dx) & 255) ^ flip), 1.0, 0.0).astype(jnp.bfloat16)
            spill = (lane < dx) | (lane >= 128 + dx)
            def merge(read):
                return jnp.concatenate([jnp.where(spill, read(0), read(edge)), read(3 - edge)], axis=1)
            return weight, merge
        weight_f, merge_f = columns(ox)
        weight_b, merge_b = columns(-ox)

        def label(z, r0, blk):
            m = m_ref[blk, z, pl.ds(r0, 8), :]
            t = t_ref[blk, z, pl.ds(r0, 8), :]
            return jnp.where((t & bit) != 0, -m, m)

        def issue_f(acc, z, t, load=None):
            r0 = 32 + oy + t * 8
            parts = [merge_f(lambda blk: f_ref[blk, z + oz, c, pl.ds(r0, 8), :]) for c in range(nc)]
            pltpu.matmul_acc_lhs(acc, jnp.concatenate(parts, axis=0).astype(jnp.bfloat16), load_staged_rhs=load)

        def issue_b(acc, z, t, load=None):
            r0 = 32 - oy + t * 8
            parts = [merge_b(lambda blk: f_ref[blk, z, c, pl.ds(r0, 8), :]) for c in range(nc)]
            lab = merge_b(lambda blk: label(z, r0, blk))
            pltpu.matmul_acc_lhs(acc, jnp.concatenate(parts + [lab, lab], axis=0).astype(jnp.bfloat16), load_staged_rhs=load)

        def consume(acc, g_ref, own, t, back):
            p = pltpu.matmul_pop(acc)
            o0 = pl.multiple_of(32 + t * 8, 8)
            g0 = pl.multiple_of(own * 64 + t * 8, 8)
            for x in range(2):
                xs = slice(x * 128, x * 128 + 128)
                q = [p[c * 8:c * 8 + 8, xs] for c in range(nc)]
                prods = [q[c] * f_ref[1 + x, own, c, pl.ds(o0, 8), :] for c in range(nc)]
                while len(prods) > 1:
                    prods = [u + v for u, v in zip(prods[::2], prods[1::2])]
                if back:
                    lab = p[nc * 8:nc * 8 + 8, xs]
                    keep = jnp.abs(lab)
                else:
                    lab = label(own, o0, 1 + x)
                    keep = m_ref[1 + x, own, pl.ds(o0, 8), :]
                s = keep * jnp.tanh(prods[0] * 0.5) + lab
                for c in range(nc):
                    g_ref[c, x, pl.ds(g0, 8), :] += s * q[c]

        pltpu.matmul_push_rhs(weight_f, 0, 0)
        pltpu.matmul_push_rhs(weight_b, 0, 1)
        issue_f(acc_f[0], lo, 0, 0)
        issue_b(acc_b[0], lo, 0, 0)
        issue_f(acc_f[1], lo, 1)
        issue_b(acc_b[1], lo, 1)

        def step(i, _):
            z = lo + lax.shift_right_logical(i, 2)
            t = (i & 3) * 2
            j = jnp.minimum(i + 1, (hi - lo) * steps - 1)
            zn = lo + lax.shift_right_logical(j, 2)
            tn = (j & 3) * 2
            for u in range(2):
                consume(acc_f[u], gf_ref, z, t + u, False)
                issue_f(acc_f[u], zn, tn + u)
                consume(acc_b[u], gb_ref, z + oz, t + u, True)
                issue_b(acc_b[u], zn, tn + u)
            return 0
        lax.fori_loop(0, (hi - lo) * steps, step, 0)
        for acc in (*acc_f, *acc_b):
            pltpu.matmul_pop(acc)

    def sweep(f0, f1, b0, b1):
        def each(k, _):
            pair(k, (f0, f1), (b0, b1))
            return 0
        lax.fori_loop(0, off_ref.shape[0], each, 0)
    forward = pltpu.ACC(0)((nc * 8, 256), jnp.float32)
    backward = pltpu.ACC(1)((nc * 8 + 16, 256), jnp.float32)
    pl.run_scoped(sweep, forward, forward, backward, backward)

    def half(i, _):
        for z in range(nz):
            for x in range(2):
                at = slice(z * 64, z * 64 + 64)
                g_ref[i, z, :, x * 128:x * 128 + 128] = (gf_ref[i, x, at] + gb_ref[i, x, at]) * 0.5
        return 0
    lax.fori_loop(0, nc, half, 0)


def affinity(off, body, side):
    _, planes, nz, tall, _ = body.shape
    nc = planes - 2
    rows = tall - 2 * HALO
    V = pl.BlockSpec(memory_space=pltpu.VMEM)
    return pl.pallas_call(
        affinity_kernel,
        out_shape=jax.ShapeDtypeStruct((nc, nz, rows, 2 * LANES), jnp.float32),
        in_specs=[pl.BlockSpec(memory_space=pltpu.SMEM), V, V],
        out_specs=V,
        scratch_shapes=[
            pltpu.VMEM((3, nz, nc, tall + PAD, LANES), jnp.float32),
            pltpu.VMEM((3, nz, tall, LANES), jnp.int32),
            pltpu.VMEM((3, nz, tall, LANES), jnp.float32),
            pltpu.VMEM((nc, 2, nz * rows + PAD, LANES), jnp.float32),
            pltpu.VMEM((nc, 2, nz * rows + PAD, LANES), jnp.float32),
        ],
        compiler_params=pltpu.CompilerParams(vmem_limit_bytes=VMEM_BYTES),
        name="affinity",
    )(off, body, side)


def on_device(embedding, offsets, targets, mask):
    return affinity(offsets, *exchange(embedding, targets, mask))


def solution(mesh):
    return jax.shard_map(
        on_device,
        mesh=mesh,
        in_specs=(P(None, None, "gy", "gx"), P(), P(None, "gy", "gx"), P(None, "gy", "gx")),
        out_specs=P(None, None, "gy", "gx"),
        check_vma=False,
    )
```

```python
import jax
import jax.numpy as jnp
from jax import lax
from jax.experimental import pallas as pl
from jax.experimental.pallas import tpu as pltpu
from jax.sharding import PartitionSpec as P

MESH = pl.DeviceIdType.MESH
HALO = 32
LANES = 128
SLOTS = LANES // HALO
LOW = 64
VMEM_BYTES = 58 << 20
PAD = 8


def roll_to(value, source, dest):
    return value if source == dest else pltpu.roll(value, (dest - source) % LANES, 1)


def exchange_kernel(e_ref, t_ref, m_ref, body_ref, side_ref, strip_ref, copied, sent, received):
    channels, slices, rows, _ = e_ref.shape
    planes = channels + 2
    groups = strip_ref.shape[1]
    me_y, me_x = lax.axis_index("gy"), lax.axis_index("gx")
    count_y, count_x = lax.axis_size("gy"), lax.axis_size("gx")
    below, above = (lax.rem(me_y + 1, count_y), me_x), (lax.rem(me_y + count_y - 1, count_y), me_x)
    right, left = (me_y, lax.rem(me_x + 1, count_x)), (me_y, lax.rem(me_x + count_x - 1, count_x))
    mine, tail, head = pl.ds(HALO, rows), pl.ds(rows, HALO), pl.ds(HALO, HALO)
    top, bottom = pl.ds(0, HALO), pl.ds(HALO + rows, HALO)

    inner, codes = pl.ds(0, channels), pl.ds(channels, 2)
    own = pltpu.make_async_copy(e_ref, body_ref.at[inner, :, mine], copied)
    own.start()

    barrier = pltpu.get_barrier_semaphore()
    for neighbour in (below, above, right, left):
        pl.semaphore_signal(barrier, inc=1, device_id=neighbour, device_id_type=MESH)
    pl.semaphore_wait(barrier, 4)

    def remote(index, source, target, device):
        copy = pltpu.make_async_remote_copy(
            src_ref=source, dst_ref=target, send_sem=sent.at[index], recv_sem=received.at[index],
            device_id=device, device_id_type=MESH,
        )
        copy.start()
        return copy

    flights = [
        remote(0, e_ref.at[:, :, pl.ds(rows - HALO, HALO)], body_ref.at[inner, :, top], below),
        remote(1, e_ref.at[:, :, pl.ds(0, HALO)], body_ref.at[inner, :, bottom], above),
    ]

    for z in range(slices):
        code = t_ref[z] | jnp.left_shift(m_ref[z], 12)
        body_ref[channels, z, HALO:HALO + rows] = (code & (LOW - 1)).astype(jnp.float32).astype(jnp.bfloat16)
        body_ref[channels + 1, z, HALO:HALO + rows] = jnp.right_shift(code, 6).astype(jnp.float32).astype(jnp.bfloat16)
    flights.append(remote(2, body_ref.at[codes, :, tail], body_ref.at[codes, :, top], below))
    flights.append(remote(3, body_ref.at[codes, :, head], body_ref.at[codes, :, bottom], above))

    own.wait()
    lane = lax.broadcasted_iota(jnp.int32, (rows, LANES), 1)
    across = []
    for x, device in ((1, right), (0, left)):
        for group in range(groups):
            packed = None
            for slot in range(SLOTS):
                c, z = divmod(group * SLOTS + slot, slices)
                columns = body_ref[c, z, HALO:HALO + rows, x * LANES:(x + 1) * LANES]
                moved = roll_to(columns, x * (LANES - HALO), slot * HALO)
                packed = moved if packed is None else jnp.where(lane >= slot * HALO, moved, packed)
            strip_ref[x, group] = packed
        across.append(remote(4 + x, strip_ref.at[x], side_ref.at[x, :, mine], device))
    for copy in across:
        copy.wait()

    corners = [
        remote(6, side_ref.at[:, :, tail], side_ref.at[:, :, top], below),
        remote(7, side_ref.at[:, :, head], side_ref.at[:, :, bottom], above),
    ]
    for copy in flights + corners:
        copy.wait()

    @pl.when(me_y == 0)
    def _():
        body_ref[:, :, 0:HALO] = jnp.zeros((planes, slices, HALO, 2 * LANES), jnp.bfloat16)
        side_ref[:, :, 0:HALO] = jnp.zeros((2, groups, HALO, LANES), jnp.bfloat16)

    @pl.when(me_y == count_y - 1)
    def _():
        body_ref[:, :, HALO + rows:] = jnp.zeros((planes, slices, HALO, 2 * LANES), jnp.bfloat16)
        side_ref[:, :, HALO + rows:] = jnp.zeros((2, groups, HALO, LANES), jnp.bfloat16)

    @pl.when(me_x == 0)
    def _():
        side_ref[1] = jnp.zeros(side_ref.shape[1:], jnp.bfloat16)

    @pl.when(me_x == count_x - 1)
    def _():
        side_ref[0] = jnp.zeros(side_ref.shape[1:], jnp.bfloat16)


def exchange(embedding, targets, mask):
    channels, slices, rows, cols = embedding.shape
    planes = channels + 2
    groups = slices * planes // SLOTS
    tall = rows + 2 * HALO
    V = pl.BlockSpec(memory_space=pltpu.VMEM)
    return pl.pallas_call(
        exchange_kernel,
        out_shape=(
            jax.ShapeDtypeStruct((planes, slices, tall, 2 * LANES), jnp.bfloat16),
            jax.ShapeDtypeStruct((2, groups, tall, LANES), jnp.bfloat16),
        ),
        in_specs=[pl.BlockSpec(memory_space=pl.ANY), V, V],
        out_specs=(V, V),
        scratch_shapes=[
            pltpu.VMEM((2, groups, rows, LANES), jnp.bfloat16),
            pltpu.SemaphoreType.DMA,
            pltpu.SemaphoreType.DMA((8,)),
            pltpu.SemaphoreType.DMA((8,)),
        ],
        compiler_params=pltpu.CompilerParams(
            collective_id=0, has_side_effects=True, vmem_limit_bytes=VMEM_BYTES
        ),
        name="exchange",
    )(embedding, targets, mask)


def affinity_kernel(off_ref, body_hbm, side_hbm, g_hbm, body_ref, side_ref, g_ref, f_ref, t_ref, m_ref, gf_ref, gb_ref,
                    arrived, stored):
    planes, nz, tall, _ = body_ref.shape
    nc = planes - 2
    tiles = (tall - 2 * HALO) // 8
    lane = lax.broadcasted_iota(jnp.int32, (8, 128), 1)
    wide = lax.broadcasted_iota(jnp.int32, (tall, LANES), 1)

    def side_copy():
        return pltpu.make_async_copy(side_hbm, side_ref, arrived.at[planes])

    def plane_copy(c):
        return pltpu.make_async_copy(body_hbm.at[c], body_ref.at[c], arrived.at[c])

    def out_copy(c):
        return pltpu.make_async_copy(g_ref.at[c], g_hbm.at[c], stored.at[c])

    side_copy().start()
    for c in range(planes):
        plane_copy(c).start()

    def zero(c, _):
        gf_ref[c] = jnp.zeros(gf_ref.shape[1:], jnp.float32)
        gb_ref[c] = jnp.zeros(gb_ref.shape[1:], jnp.float32)
        return 0
    lax.fori_loop(0, nc, zero, 0)

    def halo(c, z):
        group, slot = divmod(c * nz + z, SLOTS)
        from_right = roll_to(side_ref[0, group], slot * HALO, 0)
        from_left = roll_to(side_ref[1, group], slot * HALO, LANES - HALO)
        return jnp.where(wide < LANES // 2, from_right, from_left)

    def decode(blk, z, low, high):
        code = (low.astype(jnp.float32) + LOW * high.astype(jnp.float32)).astype(jnp.int32)
        t_ref[blk, z] = code
        m_ref[blk, z] = jnp.right_shift(code, 12).astype(jnp.float32)

    side_copy().wait()
    for c in range(nc):
        for z in range(nz):
            f_ref[0, z, c, :tall] = halo(c, z).astype(jnp.float32)
    def cast(c, _):
        plane_copy(c).wait()
        for x in range(2):
            for z in range(nz):
                f_ref[1 + x, z, c, :tall] = body_ref[c, z, :, x * LANES:(x + 1) * LANES].astype(jnp.float32)
        return 0
    lax.fori_loop(0, nc, cast, 0)
    plane_copy(nc).wait()
    plane_copy(nc + 1).wait()
    for z in range(nz):
        for x in range(2):
            at = slice(x * LANES, (x + 1) * LANES)
            decode(1 + x, z, body_ref[nc, z, :, at], body_ref[nc + 1, z, :, at])
        decode(0, z, halo(nc, z), halo(nc + 1, z))

    rows = lax.broadcasted_iota(jnp.int32, (256, 256), 0)
    cols = lax.broadcasted_iota(jnp.int32, (256, 256), 1)

    def pair(k, acc_f, acc_b):
        oz, oy, ox = off_ref[0, k], off_ref[1, k], off_ref[2, k]
        bit = jnp.left_shift(1, k)
        lo = jnp.maximum(0, -oz)
        hi = jnp.minimum(nz, nz - oz)
        steps = tiles // 2

        def columns(dx):
            edge = jnp.where(dx > 0, 1, 2)
            flip = jnp.where(dx > 0, 0, 128)
            weight = jnp.where(rows == (((cols + dx) & 255) ^ flip), 1.0, 0.0).astype(jnp.bfloat16)
            spill = (lane < dx) | (lane >= 128 + dx)
            def merge(read):
                return jnp.concatenate([jnp.where(spill, read(0), read(edge)), read(3 - edge)], axis=1)
            return weight, merge
        weight_f, merge_f = columns(ox)
        weight_b, merge_b = columns(-ox)

        def label(z, r0, blk):
            m = m_ref[blk, z, pl.ds(r0, 8), :]
            t = t_ref[blk, z, pl.ds(r0, 8), :]
            return jnp.where((t & bit) != 0, -m, m)

        def issue_f(acc, z, t, load=None):
            r0 = 32 + oy + t * 8
            parts = [merge_f(lambda blk: f_ref[blk, z + oz, c, pl.ds(r0, 8), :]) for c in range(nc)]
            pltpu.matmul_acc_lhs(acc, jnp.concatenate(parts, axis=0).astype(jnp.bfloat16), load_staged_rhs=load)

        def issue_b(acc, z, t, load=None):
            r0 = 32 - oy + t * 8
            parts = [merge_b(lambda blk: f_ref[blk, z, c, pl.ds(r0, 8), :]) for c in range(nc)]
            lab = merge_b(lambda blk: label(z, r0, blk))
            pltpu.matmul_acc_lhs(acc, jnp.concatenate(parts + [lab, lab], axis=0).astype(jnp.bfloat16), load_staged_rhs=load)

        def consume(acc, g_ref, own, t, back):
            p = pltpu.matmul_pop(acc)
            o0 = pl.multiple_of(32 + t * 8, 8)
            g0 = pl.multiple_of(own * 64 + t * 8, 8)
            for x in range(2):
                xs = slice(x * 128, x * 128 + 128)
                q = [p[c * 8:c * 8 + 8, xs] for c in range(nc)]
                prods = [q[c] * f_ref[1 + x, own, c, pl.ds(o0, 8), :] for c in range(nc)]
                while len(prods) > 1:
                    prods = [u + v for u, v in zip(prods[::2], prods[1::2])]
                if back:
                    lab = p[nc * 8:nc * 8 + 8, xs]
                    keep = jnp.abs(lab)
                else:
                    lab = label(own, o0, 1 + x)
                    keep = m_ref[1 + x, own, pl.ds(o0, 8), :]
                s = keep * jnp.tanh(prods[0] * 0.5) + lab
                for c in range(nc):
                    g_ref[c, x, pl.ds(g0, 8), :] += s * q[c]

        pltpu.matmul_push_rhs(weight_f, 0, 0)
        pltpu.matmul_push_rhs(weight_b, 0, 1)
        issue_f(acc_f[0], lo, 0, 0)
        issue_b(acc_b[0], lo, 0, 0)
        issue_f(acc_f[1], lo, 1)
        issue_b(acc_b[1], lo, 1)

        def step(i, _):
            z = lo + lax.shift_right_logical(i, 2)
            t = (i & 3) * 2
            j = jnp.minimum(i + 1, (hi - lo) * steps - 1)
            zn = lo + lax.shift_right_logical(j, 2)
            tn = (j & 3) * 2
            for u in range(2):
                consume(acc_f[u], gf_ref, z, t + u, False)
                issue_f(acc_f[u], zn, tn + u)
                consume(acc_b[u], gb_ref, z + oz, t + u, True)
                issue_b(acc_b[u], zn, tn + u)
            return 0
        lax.fori_loop(0, (hi - lo) * steps, step, 0)
        for acc in (*acc_f, *acc_b):
            pltpu.matmul_pop(acc)

    def sweep(f0, f1, b0, b1):
        def each(k, _):
            pair(k, (f0, f1), (b0, b1))
            return 0
        lax.fori_loop(0, off_ref.shape[1], each, 0)
    forward = pltpu.ACC(0)((nc * 8, 256), jnp.float32)
    backward = pltpu.ACC(1)((nc * 8 + 16, 256), jnp.float32)
    pl.run_scoped(sweep, forward, forward, backward, backward)

    def half(i, _):
        for z in range(nz):
            for x in range(2):
                at = slice(z * 64, z * 64 + 64)
                g_ref[i, z, :, x * 128:x * 128 + 128] = (gf_ref[i, x, at] + gb_ref[i, x, at]) * 0.5
        out_copy(i).start()
        return 0
    lax.fori_loop(0, nc, half, 0)

    def finish(i, _):
        out_copy(i).wait()
        return 0
    lax.fori_loop(0, nc, finish, 0)


def affinity(off, body, side):
    planes, nz, tall, _ = body.shape
    nc = planes - 2
    rows = tall - 2 * HALO
    A = pl.BlockSpec(memory_space=pl.ANY)
    return pl.pallas_call(
        affinity_kernel,
        out_shape=jax.ShapeDtypeStruct((nc, nz, rows, 2 * LANES), jnp.float32),
        in_specs=[pl.BlockSpec(memory_space=pltpu.SMEM), A, A],
        out_specs=A,
        scratch_shapes=[
            pltpu.VMEM(body.shape, body.dtype),
            pltpu.VMEM(side.shape, side.dtype),
            pltpu.VMEM((nc, nz, rows, 2 * LANES), jnp.float32),
            pltpu.VMEM((3, nz, nc, tall + PAD, LANES), jnp.float32),
            pltpu.VMEM((3, nz, tall, LANES), jnp.int32),
            pltpu.VMEM((3, nz, tall, LANES), jnp.float32),
            pltpu.VMEM((nc, 2, nz * rows + PAD, LANES), jnp.float32),
            pltpu.VMEM((nc, 2, nz * rows + PAD, LANES), jnp.float32),
            pltpu.SemaphoreType.DMA((planes + 1,)),
            pltpu.SemaphoreType.DMA((nc,)),
        ],
        compiler_params=pltpu.CompilerParams(vmem_limit_bytes=VMEM_BYTES),
        name="affinity",
    )(off, body, side)


def on_device(embedding, offsets, targets, mask):
    return affinity(offsets.T, *exchange(embedding, targets, mask))


def solution(mesh):
    return jax.shard_map(
        on_device,
        mesh=mesh,
        in_specs=(P(None, None, "gy", "gx"), P(), P(None, "gy", "gx"), P(None, "gy", "gx")),
        out_specs=P(None, None, "gy", "gx"),
        check_vma=False,
    )
```

```python
import jax
import jax.numpy as jnp
from jax import lax
from jax.experimental import pallas as pl
from jax.experimental.pallas import tpu as pltpu
from jax.sharding import PartitionSpec as P

MESH = pl.DeviceIdType.MESH
HALO = 32
LANES = 128
SLOTS = LANES // HALO
LOW = 64
VMEM_BYTES = 58 << 20
PAD = 8


def roll_to(value, source, dest):
    return value if source == dest else pltpu.roll(value, (dest - source) % LANES, 1)


def exchange_kernel(e_ref, t_ref, m_ref, body_hbm, side_hbm, body_ref, strip_ref, copied, sent, received, stored):
    channels, slices, rows, _ = e_ref.shape
    planes = channels + 2
    groups = strip_ref.shape[1]
    me_y, me_x = lax.axis_index("gy"), lax.axis_index("gx")
    count_y, count_x = lax.axis_size("gy"), lax.axis_size("gx")
    below, above = (lax.rem(me_y + 1, count_y), me_x), (lax.rem(me_y + count_y - 1, count_y), me_x)
    right, left = (me_y, lax.rem(me_x + 1, count_x)), (me_y, lax.rem(me_x + count_x - 1, count_x))
    mine, tail, head = pl.ds(HALO, rows), pl.ds(rows, HALO), pl.ds(HALO, HALO)
    top, bottom = pl.ds(0, HALO), pl.ds(HALO + rows, HALO)

    inner, codes = pl.ds(0, channels), pl.ds(channels, 2)
    own = pltpu.make_async_copy(e_ref, body_ref.at[inner], copied)
    own.start()

    barrier = pltpu.get_barrier_semaphore()
    for neighbour in (below, above, right, left):
        pl.semaphore_signal(barrier, inc=1, device_id=neighbour, device_id_type=MESH)
    pl.semaphore_wait(barrier, 4)

    def remote(index, source, target, device):
        copy = pltpu.make_async_remote_copy(
            src_ref=source, dst_ref=target, send_sem=sent.at[index], recv_sem=received.at[index],
            device_id=device, device_id_type=MESH,
        )
        copy.start()
        return copy

    flights = [
        remote(0, e_ref.at[:, :, pl.ds(rows - HALO, HALO)], body_hbm.at[inner, :, top], below),
        remote(1, e_ref.at[:, :, pl.ds(0, HALO)], body_hbm.at[inner, :, bottom], above),
    ]

    for z in range(slices):
        code = t_ref[z] | jnp.left_shift(m_ref[z], 12)
        body_ref[channels, z] = (code & (LOW - 1)).astype(jnp.float32).astype(jnp.bfloat16)
        body_ref[channels + 1, z] = jnp.right_shift(code, 6).astype(jnp.float32).astype(jnp.bfloat16)
    flights.append(remote(2, body_ref.at[codes, :, pl.ds(rows - HALO, HALO)], body_hbm.at[codes, :, top], below))
    flights.append(remote(3, body_ref.at[codes, :, pl.ds(0, HALO)], body_hbm.at[codes, :, bottom], above))

    own.wait()
    keep = pltpu.make_async_copy(body_ref, body_hbm.at[:, :, mine], stored.at[0])
    keep.start()
    lane = lax.broadcasted_iota(jnp.int32, (rows, LANES), 1)
    across = []
    for x, device in ((1, right), (0, left)):
        for group in range(groups):
            packed = None
            for slot in range(SLOTS):
                c, z = divmod(group * SLOTS + slot, slices)
                columns = body_ref[c, z, :, x * LANES:(x + 1) * LANES]
                moved = roll_to(columns, x * (LANES - HALO), slot * HALO)
                packed = moved if packed is None else jnp.where(lane >= slot * HALO, moved, packed)
            strip_ref[x, group] = packed
        across.append(remote(4 + x, strip_ref.at[x], side_hbm.at[x, :, mine], device))
    for copy in across:
        copy.wait()

    corners = [
        remote(6, side_hbm.at[:, :, tail], side_hbm.at[:, :, top], below),
        remote(7, side_hbm.at[:, :, head], side_hbm.at[:, :, bottom], above),
    ]
    for copy in flights + corners + [keep]:
        copy.wait()

    def fill(source, target):
        copy = pltpu.make_async_copy(source, target, stored.at[1])
        copy.start()
        copy.wait()

    def clear_rows(where):
        body_ref[:, :, :HALO] = jnp.zeros((planes, slices, HALO, 2 * LANES), jnp.bfloat16)
        strip_ref[:, :, :HALO] = jnp.zeros((2, groups, HALO, LANES), jnp.bfloat16)
        fill(body_ref.at[:, :, pl.ds(0, HALO)], body_hbm.at[:, :, where])
        fill(strip_ref.at[:, :, pl.ds(0, HALO)], side_hbm.at[:, :, where])

    def clear_side(which):
        strip_ref[which] = jnp.zeros((groups, rows, LANES), jnp.bfloat16)
        fill(strip_ref.at[which], side_hbm.at[which, :, mine])
        fill(strip_ref.at[which, :, pl.ds(0, HALO)], side_hbm.at[which, :, top])
        fill(strip_ref.at[which, :, pl.ds(0, HALO)], side_hbm.at[which, :, bottom])

    pl.when(me_y == 0)(lambda: clear_rows(top))
    pl.when(me_y == count_y - 1)(lambda: clear_rows(bottom))
    pl.when(me_x == 0)(lambda: clear_side(1))
    pl.when(me_x == count_x - 1)(lambda: clear_side(0))


def exchange(embedding, targets, mask):
    channels, slices, rows, cols = embedding.shape
    planes = channels + 2
    groups = slices * planes // SLOTS
    tall = rows + 2 * HALO
    A, V = pl.BlockSpec(memory_space=pl.ANY), pl.BlockSpec(memory_space=pltpu.VMEM)
    return pl.pallas_call(
        exchange_kernel,
        out_shape=(
            jax.ShapeDtypeStruct((planes, slices, tall, 2 * LANES), jnp.bfloat16),
            jax.ShapeDtypeStruct((2, groups, tall, LANES), jnp.bfloat16),
        ),
        in_specs=[A, V, V],
        out_specs=(A, A),
        scratch_shapes=[
            pltpu.VMEM((planes, slices, rows, cols), jnp.bfloat16),
            pltpu.VMEM((2, groups, rows, LANES), jnp.bfloat16),
            pltpu.SemaphoreType.DMA,
            pltpu.SemaphoreType.DMA((8,)),
            pltpu.SemaphoreType.DMA((8,)),
            pltpu.SemaphoreType.DMA((2,)),
        ],
        compiler_params=pltpu.CompilerParams(
            collective_id=0, has_side_effects=True, vmem_limit_bytes=VMEM_BYTES
        ),
        name="exchange",
    )(embedding, targets, mask)


def affinity_kernel(off_ref, body_hbm, side_hbm, g_hbm, body_ref, side_ref, g_ref, f_ref, t_ref, m_ref, gf_ref, gb_ref,
                    arrived, stored):
    planes, nz, tall, _ = body_ref.shape
    nc = planes - 2
    tiles = (tall - 2 * HALO) // 8
    lane = lax.broadcasted_iota(jnp.int32, (8, 128), 1)
    wide = lax.broadcasted_iota(jnp.int32, (tall, LANES), 1)

    def side_copy():
        return pltpu.make_async_copy(side_hbm, side_ref, arrived.at[planes])

    def plane_copy(c):
        return pltpu.make_async_copy(body_hbm.at[c], body_ref.at[c], arrived.at[c])

    def out_copy(c):
        return pltpu.make_async_copy(g_ref.at[c], g_hbm.at[c], stored.at[c])

    side_copy().start()
    for c in range(planes):
        plane_copy(c).start()

    def zero(c, _):
        gf_ref[c] = jnp.zeros(gf_ref.shape[1:], jnp.float32)
        gb_ref[c] = jnp.zeros(gb_ref.shape[1:], jnp.float32)
        return 0
    lax.fori_loop(0, nc, zero, 0)

    def halo(c, z):
        group, slot = divmod(c * nz + z, SLOTS)
        from_right = roll_to(side_ref[0, group], slot * HALO, 0)
        from_left = roll_to(side_ref[1, group], slot * HALO, LANES - HALO)
        return jnp.where(wide < LANES // 2, from_right, from_left)

    def decode(blk, z, low, high):
        code = (low.astype(jnp.float32) + LOW * high.astype(jnp.float32)).astype(jnp.int32)
        t_ref[blk, z] = code
        m_ref[blk, z] = jnp.right_shift(code, 12).astype(jnp.float32)

    side_copy().wait()
    for c in range(nc):
        for z in range(nz):
            f_ref[0, z, c, :tall] = halo(c, z).astype(jnp.float32)
    def cast(c, _):
        plane_copy(c).wait()
        for x in range(2):
            for z in range(nz):
                f_ref[1 + x, z, c, :tall] = body_ref[c, z, :, x * LANES:(x + 1) * LANES].astype(jnp.float32)
        return 0
    lax.fori_loop(0, nc, cast, 0)
    plane_copy(nc).wait()
    plane_copy(nc + 1).wait()
    for z in range(nz):
        for x in range(2):
            at = slice(x * LANES, (x + 1) * LANES)
            decode(1 + x, z, body_ref[nc, z, :, at], body_ref[nc + 1, z, :, at])
        decode(0, z, halo(nc, z), halo(nc + 1, z))

    rows = lax.broadcasted_iota(jnp.int32, (256, 256), 0)
    cols = lax.broadcasted_iota(jnp.int32, (256, 256), 1)

    def pair(k, acc_f, acc_b):
        oz, oy, ox = off_ref[0, k], off_ref[1, k], off_ref[2, k]
        bit = jnp.left_shift(1, k)
        lo = jnp.maximum(0, -oz)
        hi = jnp.minimum(nz, nz - oz)
        steps = tiles // 2

        def columns(dx):
            edge = jnp.where(dx > 0, 1, 2)
            flip = jnp.where(dx > 0, 0, 128)
            weight = jnp.where(rows == (((cols + dx) & 255) ^ flip), 1.0, 0.0).astype(jnp.bfloat16)
            spill = (lane < dx) | (lane >= 128 + dx)
            def merge(read):
                return jnp.concatenate([jnp.where(spill, read(0), read(edge)), read(3 - edge)], axis=1)
            return weight, merge
        weight_f, merge_f = columns(ox)
        weight_b, merge_b = columns(-ox)

        def label(z, r0, blk):
            m = m_ref[blk, z, pl.ds(r0, 8), :]
            t = t_ref[blk, z, pl.ds(r0, 8), :]
            return jnp.where((t & bit) != 0, -m, m)

        def issue_f(acc, z, t, load=None):
            r0 = 32 + oy + t * 8
            parts = [merge_f(lambda blk: f_ref[blk, z + oz, c, pl.ds(r0, 8), :]) for c in range(nc)]
            pltpu.matmul_acc_lhs(acc, jnp.concatenate(parts, axis=0).astype(jnp.bfloat16), load_staged_rhs=load)

        def issue_b(acc, z, t, load=None):
            r0 = 32 - oy + t * 8
            parts = [merge_b(lambda blk: f_ref[blk, z, c, pl.ds(r0, 8), :]) for c in range(nc)]
            lab = merge_b(lambda blk: label(z, r0, blk))
            pltpu.matmul_acc_lhs(acc, jnp.concatenate(parts + [lab, lab], axis=0).astype(jnp.bfloat16), load_staged_rhs=load)

        def consume(acc, g_ref, own, t, back):
            p = pltpu.matmul_pop(acc)
            o0 = pl.multiple_of(32 + t * 8, 8)
            g0 = pl.multiple_of(own * 64 + t * 8, 8)
            for x in range(2):
                xs = slice(x * 128, x * 128 + 128)
                q = [p[c * 8:c * 8 + 8, xs] for c in range(nc)]
                prods = [q[c] * f_ref[1 + x, own, c, pl.ds(o0, 8), :] for c in range(nc)]
                while len(prods) > 1:
                    prods = [u + v for u, v in zip(prods[::2], prods[1::2])]
                if back:
                    lab = p[nc * 8:nc * 8 + 8, xs]
                    keep = jnp.abs(lab)
                else:
                    lab = label(own, o0, 1 + x)
                    keep = m_ref[1 + x, own, pl.ds(o0, 8), :]
                s = keep * jnp.tanh(prods[0] * 0.5) + lab
                for c in range(nc):
                    g_ref[c, x, pl.ds(g0, 8), :] += s * q[c]

        pltpu.matmul_push_rhs(weight_f, 0, 0)
        pltpu.matmul_push_rhs(weight_b, 0, 1)
        issue_f(acc_f[0], lo, 0, 0)
        issue_b(acc_b[0], lo, 0, 0)
        issue_f(acc_f[1], lo, 1)
        issue_b(acc_b[1], lo, 1)

        def step(i, _):
            z = lo + lax.shift_right_logical(i, 2)
            t = (i & 3) * 2
            j = jnp.minimum(i + 1, (hi - lo) * steps - 1)
            zn = lo + lax.shift_right_logical(j, 2)
            tn = (j & 3) * 2
            for u in range(2):
                consume(acc_f[u], gf_ref, z, t + u, False)
                issue_f(acc_f[u], zn, tn + u)
                consume(acc_b[u], gb_ref, z + oz, t + u, True)
                issue_b(acc_b[u], zn, tn + u)
            return 0
        lax.fori_loop(0, (hi - lo) * steps, step, 0)
        for acc in (*acc_f, *acc_b):
            pltpu.matmul_pop(acc)

    def sweep(f0, f1, b0, b1):
        def each(k, _):
            pair(k, (f0, f1), (b0, b1))
            return 0
        lax.fori_loop(0, off_ref.shape[1], each, 0)
    forward = pltpu.ACC(0)((nc * 8, 256), jnp.float32)
    backward = pltpu.ACC(1)((nc * 8 + 16, 256), jnp.float32)
    pl.run_scoped(sweep, forward, forward, backward, backward)

    def half(i, _):
        for z in range(nz):
            for x in range(2):
                at = slice(z * 64, z * 64 + 64)
                g_ref[i, z, :, x * 128:x * 128 + 128] = (gf_ref[i, x, at] + gb_ref[i, x, at]) * 0.5
        out_copy(i).start()
        return 0
    lax.fori_loop(0, nc, half, 0)

    def finish(i, _):
        out_copy(i).wait()
        return 0
    lax.fori_loop(0, nc, finish, 0)


def affinity(off, body, side):
    planes, nz, tall, _ = body.shape
    nc = planes - 2
    rows = tall - 2 * HALO
    A = pl.BlockSpec(memory_space=pl.ANY)
    return pl.pallas_call(
        affinity_kernel,
        out_shape=jax.ShapeDtypeStruct((nc, nz, rows, 2 * LANES), jnp.float32),
        in_specs=[pl.BlockSpec(memory_space=pltpu.SMEM), A, A],
        out_specs=A,
        scratch_shapes=[
            pltpu.VMEM(body.shape, body.dtype),
            pltpu.VMEM(side.shape, side.dtype),
            pltpu.VMEM((nc, nz, rows, 2 * LANES), jnp.float32),
            pltpu.VMEM((3, nz, nc, tall + PAD, LANES), jnp.float32),
            pltpu.VMEM((3, nz, tall, LANES), jnp.int32),
            pltpu.VMEM((3, nz, tall, LANES), jnp.float32),
            pltpu.VMEM((nc, 2, nz * rows + PAD, LANES), jnp.float32),
            pltpu.VMEM((nc, 2, nz * rows + PAD, LANES), jnp.float32),
            pltpu.SemaphoreType.DMA((planes + 1,)),
            pltpu.SemaphoreType.DMA((nc,)),
        ],
        compiler_params=pltpu.CompilerParams(vmem_limit_bytes=VMEM_BYTES),
        name="affinity",
    )(off, body, side)


def on_device(embedding, offsets, targets, mask):
    return affinity(offsets.T, *exchange(embedding, targets, mask))


def solution(mesh):
    return jax.shard_map(
        on_device,
        mesh=mesh,
        in_specs=(P(None, None, "gy", "gx"), P(), P(None, "gy", "gx"), P(None, "gy", "gx")),
        out_specs=P(None, None, "gy", "gx"),
        check_vma=False,
    )
```
